32 devices in a mesh: groups: 2 (over y), ctx: 4 (over z), exp: 4 (over x, core).
Axes of the slice: x: 2, y: 2, z: 4, core: 2. Of those that a mesh axis runs over, the one named last changes fastest.
Arguments:
- tokens: bfloat16 [1024, 2048], P(('groups', 'ctx')), parts along dimension 0, may hold values from -6 to 6
- positions: int32 [1024], P(('groups', 'ctx')), parts along dimension 0, may hold values from 0 to 511, as said below
- attn_gain: float32 [2048], replicated, may hold values from 0.1 to 1.9
- w_qkv: bfloat16 [2048, 16, 384], P(None, 'exp')
- w_out: bfloat16 [16, 128, 2048], P('exp'), may hold values from -0.5 to 0.5
- moe_gain: float32 [2048], replicated, may hold values from 0.1 to 1.9
- expert_ids: int32 [1024, 6], P(('groups', 'ctx', 'exp')), parts along dimension 0, may hold values from 0 to 63, as said below
- gate_probs: float32 [1024, 6], P(('groups', 'ctx', 'exp')), parts along dimension 0, may hold values from 0.1 to 1
- w_gate: bfloat16 [4, 2048, 768], P('exp', 'ctx'), may hold values from -0.125 to 0.125
- w_up: bfloat16 [4, 2048, 768], P('exp', 'ctx'), may hold values from -0.125 to 0.125
- w_down: bfloat16 [4, 768, 2048], P('exp', None, 'ctx'), may hold values from -0.21875 to 0.21875
Outputs:
- mixed: bfloat16 [1024, 2048], P(('groups', 'ctx', 'exp')), parts along dimension 0
The draws below stay inside these ranges and needn't reach their ends.
There are 2 independent parts, one for each index of `groups`. The reference program is written for one: setup_inputs(seed, part) draws one part's arguments, and reference() takes and returns one part's arrays. A program takes and returns all parts, laid end to end along the dimension named above; an argument that names none is the same for every part. Nothing has to cross between parts.
Inputs may be any that keep to these rules, and one draw needn't show every extreme that they name: `positions`: each of 0 to 511 once: a prefix in order, then a suffix in order, then the middle in order. `expert_ids`: each row names 6 different experts; in each aligned block of 32 rows (the rows of one device) no expert is named by more than 6 rows, and one expert below 4 is named by exactly 6 rows in every block.
All inputs are finite; a program needn't handle non-finite values.
Results may differ from the reference program's by a relative error of at most 0.011.
Values may be sent and summed in bfloat16 or wider, within the bound.
A program may use at most 128 MiB of HBM per device.

```python
import math
import jax
import jax.numpy as jnp
from jax import lax

D = 2048
HEADS = 16
HD = 128
ROUTED = 64
TOP = 6
FF_E = 768
TOKM = 32
CAP = 6
FLIGHT = 4
HEAD_GROUP = 4
SEQ_DEV = 128
SEQ = 512
N_CTX = 4
N_EXP = 4


def draw_positions(key, part):
    key = jax.random.fold_in(key, 11)
    first_key, second_key = jax.random.split(key)
    start = jax.random.randint(first_key, (), 1, SEQ // 2)
    finish = jax.random.randint(second_key, (), SEQ // 2 + 1, SEQ)
    order = jnp.arange(SEQ, dtype=jnp.int32)
    tail = SEQ - finish
    middle = jnp.where(order < start + tail, finish + order - start, order - tail)
    return jnp.where(order < start, order, middle).astype(jnp.int32)


def draw_w_qkv(key, part):
    key = jax.random.fold_in(key, 23)
    query_key, key_key, value_key = jax.random.split(key, 3)
    shape = (D, HEADS, HD)
    root = 1.0 / math.sqrt(D)
    query = jax.random.normal(query_key, shape, jnp.float32) * (1.41 * root)
    key_part = jax.random.normal(key_key, shape, jnp.float32) * (1.41 * root)
    values = jax.random.normal(value_key, shape, jnp.float32) * root
    return jnp.concatenate([query, key_part, values], axis=2).astype(jnp.bfloat16)


def draw_expert_ids(key, part):
    key = jax.random.fold_in(key, 37)
    pick_key, lean_key, score_key, row_key = jax.random.split(key, 4)
    forced = jax.random.randint(pick_key, (), 0, FLIGHT)
    blocks = SEQ // TOKM
    lean = jax.random.randint(lean_key, (ROUTED,), 0, 4)
    noise = jax.random.randint(score_key, (blocks, TOKM, ROUTED), 0, 1024)
    experts = jnp.arange(ROUTED, dtype=jnp.int32)
    ranking = ((lean[None, None, :] * 1024 + noise) * ROUTED + experts[None, None, :]).astype(jnp.int32)
    row_keys = jax.random.split(row_key, blocks)

    def forced_rows(block_key):
        shuffled = jax.random.permutation(block_key, TOKM)
        return jnp.zeros((TOKM,), jnp.int32).at[shuffled[:CAP]].set(1)
    marked = jax.vmap(forced_rows)(row_keys)

    def fill_block(block_ranking, block_marked):

        def place_row(counts, inputs):
            row_ranking, must = inputs
            score = jnp.where(counts < CAP, row_ranking, -1)
            score = jnp.where(experts == forced, jnp.where(must > 0, 1 << 30, -2), score)
            picked = lax.top_k(score, TOP)[1].astype(jnp.int32)
            counts = counts + jnp.sum((picked[:, None] == experts[None, :]).astype(jnp.int32), axis=0)
            return (counts, picked)
        return lax.scan(place_row, jnp.zeros((ROUTED,), jnp.int32), (block_ranking, block_marked))[1]
    return jax.vmap(fill_block)(ranking, marked).reshape(SEQ, TOP).astype(jnp.int32)


def levels(key, extent, pieces, smallest, largest):
    level, own = 1.0, jax.random.fold_in(key, 6)
    for dim, blocks in pieces:
        steps = jnp.exp(jax.random.uniform(jax.random.fold_in(own, dim), (blocks,), jnp.float32, smallest / len(pieces), largest / len(pieces)))
        level = level * jnp.repeat(steps, extent[dim] // blocks).reshape([-1 if axis == dim else 1 for axis in range(len(extent))])
    return level


def normal_values(key, shape, scale, limit, pieces=(), held_as=jnp.bfloat16):
    factor_of = levels(key, shape, pieces, -0.22, 0.18) if pieces else 1.0
    values = jax.random.normal(key, shape, jnp.float32) * scale * factor_of
    return jnp.minimum(jnp.maximum(values, -limit), limit).astype(held_as)


def setup_inputs(seed: int = 0, part: int = 0) -> dict:
    streams_of = jax.random.split(jax.random.key(seed), 12)
    part_keys = jax.random.split(jax.random.fold_in(streams_of[11], part), 12)
    tokens = normal_values(part_keys[0], (SEQ, D), 1.0, 6.0, ((0, 4),))
    positions = draw_positions(jax.random.fold_in(jax.random.fold_in(streams_of[11], part), 71), part)
    attn_gain = jnp.clip(1.0 + 0.18 * jax.random.normal(streams_of[2], (D,), jnp.float32), 0.1, 1.9)
    w_qkv = draw_w_qkv(jax.random.fold_in(streams_of[11], 71), part)
    w_out = normal_values(streams_of[4], (HEADS, HD, D), HD ** -0.5, 0.5, ((0, 4),))
    moe_gain = jnp.clip(1.0 + 0.18 * jax.random.normal(streams_of[5], (D,), jnp.float32), 0.1, 1.9)
    expert_ids = draw_expert_ids(jax.random.fold_in(jax.random.fold_in(streams_of[11], part), 71), part)
    gate_probs = jnp.clip(jnp.exp(math.log(1.0) - 2.3025851 * jax.random.uniform(part_keys[7], (SEQ, TOP), jnp.float32) ** levels(part_keys[7], (SEQ, TOP), ((0, 16),), -0.2, 0.2)), 0.1, 1.0)
    w_gate = normal_values(streams_of[8], (FLIGHT, D, FF_E), D ** -0.5, 0.125, ((0, 4), (1, 4)))
    w_up = normal_values(streams_of[9], (FLIGHT, D, FF_E), D ** -0.5, 0.125, ((0, 4), (1, 4)))
    w_down = normal_values(streams_of[10], (FLIGHT, FF_E, D), FF_E ** -0.5, 0.21875, ((0, 4), (2, 4)))
    return dict(tokens=tokens, positions=positions, attn_gain=attn_gain, w_qkv=w_qkv, w_out=w_out, moe_gain=moe_gain, expert_ids=expert_ids, gate_probs=gate_probs, w_gate=w_gate, w_up=w_up, w_down=w_down)


epsilon = 1e-06

def rms_norm(rows, gain):
    rows = rows.astype(jnp.float32)
    return rows * lax.rsqrt(lax.optimization_barrier(jnp.mean(rows * rows, axis=-1, keepdims=True)) + epsilon) * gain

def rotary_tables(positions, width):
    freqs = 10000.0 ** (-jnp.arange(width // 2, dtype=jnp.float32) * 2.0 / width)
    angles = positions.astype(jnp.float32)[:, None] * freqs[None, :]
    return (jnp.cos(angles), jnp.sin(angles))

def rotate(vectors, cosines, sines):
    half = vectors.shape[-1] // 2
    first = vectors[..., :half]
    second = vectors[..., half:]
    return jnp.concatenate([first * cosines - second * sines, second * cosines + first * sines], axis=-1)

def reference(tokens, positions, attn_gain, w_qkv, w_out, moe_gain, expert_ids, gate_probs, w_gate, w_up, w_down):
    normed = rms_norm(tokens, attn_gain).astype(jnp.bfloat16)
    cosines, sines = rotary_tables(positions, HD)
    order = jnp.arange(SEQ, dtype=jnp.int32)
    blocks = SEQ // SEQ_DEV

    def one_head(head):
        weights = lax.dynamic_index_in_dim(w_qkv, head, 1, keepdims=False)
        projected = jnp.dot(normed.astype(jnp.float32), weights.astype(jnp.float32), preferred_element_type=jnp.float32)
        queries = rotate(projected[:, :HD], cosines, sines).astype(jnp.bfloat16)
        key_rows = rotate(projected[:, HD:2 * HD], cosines, sines).astype(jnp.bfloat16)
        value_rows = projected[:, 2 * HD:].astype(jnp.bfloat16)

        def one_block(index):
            rows = lax.dynamic_slice_in_dim(queries, index * SEQ_DEV, SEQ_DEV, 0)
            scores = jnp.dot(rows.astype(jnp.float32), key_rows.astype(jnp.float32).T, preferred_element_type=jnp.float32) * HD ** (-0.5)
            mine = lax.dynamic_slice_in_dim(order, index * SEQ_DEV, SEQ_DEV, 0)
            scores = jnp.where(order[None, :] <= mine[:, None], scores, -jnp.inf)
            peak = lax.optimization_barrier(jnp.max(scores, axis=1, keepdims=True))
            probs = jnp.exp(scores - peak)
            total = lax.optimization_barrier(jnp.sum(probs, axis=1, keepdims=True))
            weighted = jnp.dot(probs.astype(jnp.bfloat16).astype(jnp.float32), value_rows.astype(jnp.float32), preferred_element_type=jnp.float32)
            return (weighted / total).astype(jnp.bfloat16)
        return lax.map(one_block, jnp.arange(blocks, dtype=jnp.int32)).reshape(SEQ, HD)
    heads_out = lax.map(one_head, jnp.arange(HEADS, dtype=jnp.int32))

    def add_group(total, index):
        outs = lax.dynamic_slice_in_dim(heads_out, index * HEAD_GROUP, HEAD_GROUP, 0).astype(jnp.float32)
        project = lax.dynamic_slice_in_dim(w_out, index * HEAD_GROUP, HEAD_GROUP, 0).astype(jnp.float32)
        term = jnp.einsum('hsc,hcd->sd', outs, project).astype(jnp.bfloat16)
        term = lax.optimization_barrier(term).astype(jnp.float32)
        return (total + term, None)
    attn_sum, _ = lax.scan(add_group, jnp.zeros((SEQ, D), jnp.float32), jnp.arange(HEADS // HEAD_GROUP, dtype=jnp.int32))
    residual = tokens.astype(jnp.float32) + attn_sum
    normed_moe = rms_norm(residual, moe_gain).astype(jnp.bfloat16)
    bound_rows = N_CTX * N_EXP * CAP

    def add_expert(total, expert):
        hits = expert_ids == expert
        chosen = jnp.any(hits, axis=1)
        weight = lax.optimization_barrier(jnp.sum(jnp.where(hits, gate_probs, 0.0), axis=1))
        picked = jnp.nonzero(chosen, size=bound_rows, fill_value=0)[0].astype(jnp.int32)
        valid = jnp.arange(bound_rows, dtype=jnp.int32) < jnp.sum(chosen.astype(jnp.int32))
        rows = normed_moe[picked].astype(jnp.float32)
        gate_sum = jnp.dot(rows, w_gate[expert].astype(jnp.float32), preferred_element_type=jnp.float32)
        up_sum = jnp.dot(rows, w_up[expert].astype(jnp.float32), preferred_element_type=jnp.float32)
        hidden = (jax.nn.silu(gate_sum) * up_sum).astype(jnp.bfloat16)
        hidden = lax.optimization_barrier(hidden).astype(jnp.float32)
        result = jnp.dot(hidden, w_down[expert].astype(jnp.float32), preferred_element_type=jnp.float32).astype(jnp.bfloat16)
        result = lax.optimization_barrier(result).astype(jnp.float32)
        scaled = jnp.where(valid, weight[picked], 0.0)[:, None] * result
        return (total.at[picked].add(scaled), None)
    moe_sum, _ = lax.scan(add_expert, jnp.zeros((SEQ, D), jnp.float32), jnp.arange(FLIGHT, dtype=jnp.int32))
    return (residual + moe_sum).astype(jnp.bfloat16)
```

```python
import jax
import jax.numpy as jnp
from jax import lax
from jax.sharding import PartitionSpec as P

CAP = 6


epsilon = 1e-06


def rms_norm(rows, gain):
    rows = rows.astype(jnp.float32)
    return rows * lax.rsqrt(jnp.mean(rows * rows, axis=-1, keepdims=True) + epsilon) * gain


def rotary_tables(positions, width):
    freqs = 10000.0 ** (-jnp.arange(width // 2, dtype=jnp.float32) * 2.0 / width)
    angles = positions.astype(jnp.float32)[:, None] * freqs[None, :]
    return (jnp.cos(angles), jnp.sin(angles))


def rotate(vectors, cosines, sines):
    half = vectors.shape[-1] // 2
    first = vectors[..., :half]
    second = vectors[..., half:]
    return jnp.concatenate(
        [first * cosines - second * sines, second * cosines + first * sines], axis=-1
    )


def update(carry, pieces, rows, row_order, scale):
    peak, total, summed = carry
    key_piece, value_piece = pieces
    scores = jnp.einsum("hqc,hkc->hqk", rows, key_piece, preferred_element_type=jnp.float32) * scale
    key_order = jnp.arange(key_piece.shape[1], dtype=jnp.int32)
    allowed = key_order[None, :] <= row_order[:, None]
    scores = jnp.where(allowed[None], scores, -jnp.inf)
    new_peak = jnp.max(scores, axis=2)
    safe_peak = jnp.where(jnp.isfinite(new_peak), new_peak, 0.0)
    probs = jnp.exp(scores - safe_peak[..., None])
    factor = jnp.exp(peak - safe_peak)
    weights = probs.astype(jnp.bfloat16)
    summed = summed * factor[..., None] + jnp.einsum(
        "hqk,hkc->hqc", weights, value_piece, preferred_element_type=jnp.float32
    )
    total = total * factor + jnp.sum(probs, axis=2)
    return (new_peak, total, summed)


def empty_state(heads_here, rows_count, head_dim):
    return (
        jnp.full((heads_here, rows_count), -jnp.inf, jnp.float32),
        jnp.zeros((heads_here, rows_count), jnp.float32),
        jnp.zeros((heads_here, rows_count, head_dim), jnp.float32),
    )


def body(
    tokens,
    positions,
    attn_gain,
    w_qkv,
    w_out,
    moe_gain,
    expert_ids,
    gate_probs,
    w_gate,
    w_up,
    w_down,
):
    seq_dev = tokens.shape[0]
    width = tokens.shape[1]
    head_dim = w_out.shape[1]
    heads_here = w_out.shape[0]
    normed = rms_norm(tokens, attn_gain).astype(jnp.bfloat16)
    projected = jnp.einsum("sd,dhc->hsc", normed, w_qkv, preferred_element_type=jnp.float32)
    cosines, sines = rotary_tables(positions, head_dim)
    queries = rotate(projected[..., :head_dim], cosines, sines).astype(jnp.bfloat16)
    key_rows = rotate(projected[..., head_dim : 2 * head_dim], cosines, sines).astype(jnp.bfloat16)
    value_rows = projected[..., 2 * head_dim :].astype(jnp.bfloat16)
    first_query = lax.axis_index("ctx") * seq_dev
    query_order = first_query + jnp.arange(seq_dev, dtype=jnp.int32)
    scale = head_dim ** (-0.5)
    init = empty_state(heads_here, seq_dev, head_dim)
    folded = update(
        init,
        (
            lax.all_gather(key_rows, "ctx", axis=1, tiled=True),
            lax.all_gather(value_rows, "ctx", axis=1, tiled=True),
        ),
        queries,
        query_order,
        scale,
    )
    attended = (folded[2] / folded[1][..., None]).astype(jnp.bfloat16)
    exp_rows = seq_dev // lax.axis_size("exp")
    attn_rows = lax.psum_scatter(
        jnp.einsum("hsc,hcd->sd", attended, w_out, preferred_element_type=jnp.float32).astype(
            jnp.bfloat16
        ),
        "exp",
        scatter_dimension=0,
        tiled=True,
    ).astype(jnp.float32)
    own_tokens = lax.dynamic_slice_in_dim(
        tokens, lax.axis_index("exp") * exp_rows, exp_rows, 0
    ).astype(jnp.float32)
    residual = own_tokens + attn_rows
    normed_moe = rms_norm(residual, moe_gain).astype(jnp.bfloat16)
    flight = lax.axis_size("exp")
    slot_count = flight * CAP
    flat_ids = expert_ids.reshape(-1)
    in_flight = flat_ids < flight
    expert_marks = (
        (flat_ids[:, None] == jnp.arange(flight, dtype=jnp.int32)[None, :]) & in_flight[:, None]
    ).astype(jnp.int32)
    earlier = jnp.cumsum(expert_marks, axis=0) - expert_marks
    place_in = jnp.sum(earlier * expert_marks, axis=1)
    slot_of = jnp.where(in_flight, flat_ids * CAP + place_in, -1).reshape(expert_ids.shape)
    slot_hits = slot_of[:, :, None] == jnp.arange(slot_count, dtype=jnp.int32)[None, None, :]
    send_matrix = jnp.sum(slot_hits.astype(jnp.int32), axis=1).astype(jnp.bfloat16)
    combine_matrix = jnp.sum(jnp.where(slot_hits, gate_probs[:, :, None], 0.0), axis=1)
    outgoing = jnp.einsum(
        "ts,td->sd", send_matrix, normed_moe, preferred_element_type=jnp.float32
    ).astype(jnp.bfloat16)
    n_ctx = lax.axis_size("ctx")
    columns = width // n_ctx
    by_device = outgoing.reshape(flight, CAP, n_ctx, columns).transpose(2, 0, 1, 3)
    incoming = lax.all_to_all(
        by_device.reshape(n_ctx * flight, CAP, columns),
        ("ctx", "exp"),
        split_axis=0,
        concat_axis=0,
        tiled=True,
    )
    routed_rows = incoming.reshape(-1, columns)
    gate_up = jnp.dot(
        routed_rows,
        jnp.concatenate([w_gate[0], w_up[0]], axis=1),
        preferred_element_type=jnp.float32,
    )
    gate_up = lax.psum_scatter(gate_up, "ctx", scatter_dimension=0, tiled=True)
    hidden_width = w_gate.shape[2]
    hidden = (jax.nn.silu(gate_up[:, :hidden_width]) * gate_up[:, hidden_width:]).astype(
        jnp.bfloat16
    )
    expert_out = jnp.dot(
        lax.all_gather(hidden, "ctx", axis=0, tiled=True),
        w_down[0],
        preferred_element_type=jnp.float32,
    ).astype(jnp.bfloat16)
    returned = lax.all_to_all(
        expert_out.reshape(n_ctx * flight, CAP, columns),
        ("ctx", "exp"),
        split_axis=0,
        concat_axis=0,
        tiled=True,
    )
    returned = returned.reshape(n_ctx, flight, CAP, columns).transpose(1, 2, 0, 3)
    moe_sum = jnp.dot(
        combine_matrix,
        returned.reshape(slot_count, width).astype(jnp.float32),
        precision=lax.Precision.HIGHEST,
    )
    return (residual + moe_sum).astype(jnp.bfloat16)


def solution(mesh):
    return jax.shard_map(
        body,
        mesh=mesh,
        in_specs=(
            P(("groups", "ctx"), None),
            P(("groups", "ctx")),
            P(),
            P(None, "exp", None),
            P("exp", None, None),
            P(),
            P(("groups", "ctx", "exp"), None),
            P(("groups", "ctx", "exp"), None),
            P("exp", "ctx", None),
            P("exp", "ctx", None),
            P("exp", None, "ctx"),
        ),
        out_specs=P(("groups", "ctx", "exp"), None),
        check_vma=False,
    )
```

```python
import functools

import jax
import jax.numpy as jnp
from jax import lax
from jax.experimental import pallas as pl
from jax.experimental.pallas import tpu as pltpu
from jax.sharding import PartitionSpec as P

CAP = 6
ROWS = 8


epsilon = 1e-06


def rms_norm(rows, gain):
    rows = rows.astype(jnp.float32)
    return rows * lax.rsqrt(jnp.mean(rows * rows, axis=-1, keepdims=True) + epsilon) * gain


def rotary_tables(positions, width):
    freqs = 10000.0 ** (-jnp.arange(width // 2, dtype=jnp.float32) * 2.0 / width)
    angles = positions.astype(jnp.float32)[:, None] * freqs[None, :]
    return (jnp.cos(angles), jnp.sin(angles))


def rotate(vectors, cosines, sines):
    half = vectors.shape[-1] // 2
    first = vectors[..., :half]
    second = vectors[..., half:]
    return jnp.concatenate(
        [first * cosines - second * sines, second * cosines + first * sines], axis=-1
    )


def layer_kernel(
    n_ctx,
    n_exp,
    pieces,
    q_ref,
    kv_ref,
    tokens_ref,
    gain_ref,
    send_matrix_ref,
    combine_ref,
    w_out_hbm,
    w_gate_hbm,
    w_up_hbm,
    w_down_hbm,
    out_ref,
    kv_buf,
    peak_ref,
    total_ref,
    sum_ref,
    attended_ref,
    w_out,
    w_gate,
    w_up,
    w_down,
    rs_send,
    rs_recv,
    rows_send,
    rows_recv,
    part_send,
    part_recv,
    hidden_ref,
    back_send,
    back_recv,
    weight_sem,
    kv_send_sem,
    kv_recv_sem,
    rs_send_sem,
    rs_recv_sem,
    rows_send_sem,
    rows_recv_sem,
    part_send_sem,
    part_recv_sem,
    hidden_send_sem,
    hidden_recv_sem,
    back_send_sem,
    back_recv_sem,
):
    f32 = jnp.float32
    bf16 = jnp.bfloat16
    devices = n_ctx * n_exp
    c = lax.axis_index("ctx")
    e = lax.axis_index("exp")
    me = c * n_exp + e
    heads, seq, head_dim = q_ref.shape
    own, width = tokens_ref.shape
    columns = width // n_ctx
    piece = columns // pieces
    hidden_width = w_gate.shape[1]

    loads = [
        pltpu.make_async_copy(w_out_hbm, w_out, weight_sem.at[0]),
        pltpu.make_async_copy(w_gate_hbm, w_gate, weight_sem.at[1]),
        pltpu.make_async_copy(w_up_hbm, w_up, weight_sem.at[2]),
        pltpu.make_async_copy(w_down_hbm, w_down, weight_sem.at[3]),
    ]
    for load in loads:
        load.start()

    barrier = pltpu.get_barrier_semaphore()

    def greet(k, carry):
        peer = lax.rem(me + k, devices)
        pl.semaphore_signal(
            barrier,
            inc=1,
            device_id={"ctx": peer // n_exp, "exp": lax.rem(peer, n_exp)},
            device_id_type=pl.DeviceIdType.MESH,
        )
        return carry

    lax.fori_loop(1, devices, greet, 0)
    pl.semaphore_wait(barrier, devices - 1)

    def remote(src, dst, send_sem, recv_sem, device):
        return pltpu.make_async_remote_copy(
            src_ref=src,
            dst_ref=dst,
            send_sem=send_sem,
            recv_sem=recv_sem,
            device_id=device,
            device_id_type=pl.DeviceIdType.MESH,
        )

    def hop(source, block):
        return remote(
            source,
            kv_buf.at[block],
            kv_send_sem.at[block],
            kv_recv_sem.at[block],
            {"ctx": lax.rem(c + 1, n_ctx)},
        )

    @pl.when(c + 1 < n_ctx)
    def _():
        hop(kv_ref, c).start()

    scale = head_dim ** (-0.5)
    over_last = (((1,), (1,)), ((), ()))
    allowed = lax.broadcasted_iota(jnp.int32, (seq, seq), 1) <= lax.broadcasted_iota(
        jnp.int32, (seq, seq), 0
    )
    for head in range(heads):
        scores = (
            lax.dot_general(q_ref[head], kv_ref[head], over_last, preferred_element_type=f32)
            * scale
        )
        scores = jnp.where(allowed, scores, -jnp.inf)
        peak = jnp.max(scores, axis=1, keepdims=True)
        probs = jnp.exp(scores - peak)
        peak_ref[head] = peak
        total_ref[head] = jnp.sum(probs, axis=1, keepdims=True)
        sum_ref[head] = jnp.dot(
            probs.astype(bf16), kv_ref[heads + head], preferred_element_type=f32
        )

    def earlier_block(step, carry):
        @pl.when(step <= c)
        def _():
            block = c - step
            hop(kv_buf.at[block], block).wait_recv()

            @pl.when(c + 1 < n_ctx)
            def _():
                hop(kv_buf.at[block], block).start()

            for head in range(heads):
                scores = (
                    lax.dot_general(
                        q_ref[head], kv_buf[block, head], over_last, preferred_element_type=f32
                    )
                    * scale
                )
                old_peak = peak_ref[head]
                peak = jnp.maximum(old_peak, jnp.max(scores, axis=1, keepdims=True))
                probs = jnp.exp(scores - peak)
                factor = jnp.exp(old_peak - peak)
                peak_ref[head] = peak
                total_ref[head] = total_ref[head] * factor + jnp.sum(probs, axis=1, keepdims=True)
                sum_ref[head] = sum_ref[head] * factor + jnp.dot(
                    probs.astype(bf16), kv_buf[block, heads + head], preferred_element_type=f32
                )

        return carry

    lax.fori_loop(1, n_ctx, earlier_block, 0)
    for head in range(heads):
        attended_ref[:, head * head_dim : (head + 1) * head_dim] = (
            sum_ref[head] / total_ref[head]
        ).astype(bf16)

    loads[0].wait()
    chunk = 512
    for start in range(0, width, chunk):
        part = jnp.dot(
            attended_ref[...], w_out[:, start : start + chunk], preferred_element_type=f32
        )
        rs_send[:, :, start : start + chunk] = part.astype(bf16).reshape(n_exp, own, chunk)

    def share(k):
        peer = lax.rem(e + k, n_exp)
        return remote(
            rs_send.at[peer],
            rs_recv.at[k],
            rs_send_sem.at[k],
            rs_recv_sem.at[k],
            {"exp": peer},
        )

    def start_of(copy_of):
        def step(k, carry):
            copy_of(k).start()
            return carry

        return step

    def wait_recv_of(copy_of):
        def step(k, carry):
            copy_of(k).wait_recv()
            return carry

        return step

    def wait_send_of(copy_of):
        def step(k, carry):
            copy_of(k).wait_send()
            return carry

        return step

    lax.fori_loop(1, n_exp, start_of(share), 0)
    residual = tokens_ref[...].astype(f32) + rs_send[e].astype(f32)
    lax.fori_loop(1, n_exp, wait_recv_of(share), 0)
    for k in range(1, n_exp):
        residual = residual + rs_recv[k].astype(f32)

    square = jnp.mean(residual * residual, axis=-1, keepdims=True)
    normed = (residual * lax.rsqrt(square + epsilon) * gain_ref[...]).astype(bf16)
    outgoing = jnp.dot(send_matrix_ref[...], normed, preferred_element_type=f32)

    def packed(rows):
        parts = [
            rows[:, p * piece : (p + 1) * piece].reshape(-1, ROWS, piece) for p in range(pieces)
        ]
        if pieces == 1:
            parts.append(jnp.zeros_like(parts[0]))
        return jnp.concatenate(parts, axis=1).astype(bf16)

    def unpacked(rows, p):
        return rows[:, p * ROWS : (p + 1) * ROWS, :].reshape(-1, piece)

    for block in range(n_ctx):
        rows_send[block * n_exp : (block + 1) * n_exp] = packed(
            outgoing[:, block * columns : (block + 1) * columns]
        )

    def to_all(send, recv, send_sem, recv_sem):
        def copy_of(k):
            peer = lax.rem(me + k, devices)
            return remote(
                send.at[peer],
                recv.at[me],
                send_sem.at[k],
                recv_sem.at[k],
                {"ctx": peer // n_exp, "exp": lax.rem(peer, n_exp)},
            )

        return copy_of

    dispatch = to_all(rows_send, rows_recv, rows_send_sem, rows_recv_sem)
    lax.fori_loop(1, devices, start_of(dispatch), 0)
    rows_recv[me] = rows_send[me]
    loads[1].wait()
    loads[2].wait()
    lax.fori_loop(1, devices, wait_recv_of(dispatch), 0)
    incoming = rows_recv[...].astype(f32)
    gate = None
    for p in range(pieces):
        rows = unpacked(incoming, p).astype(bf16)
        gate_p = jnp.dot(
            rows, w_gate[p * piece : (p + 1) * piece, :], preferred_element_type=f32
        )
        up_p = jnp.dot(rows, w_up[p * piece : (p + 1) * piece, :], preferred_element_type=f32)
        gate, up = (gate_p, up_p) if gate is None else (gate + gate_p, up + up_p)
    part_send[:, :, :hidden_width] = gate.astype(bf16).reshape(n_ctx, -1, hidden_width)
    part_send[:, :, hidden_width:] = up.astype(bf16).reshape(n_ctx, -1, hidden_width)

    def partial(k):
        peer = lax.rem(c + k, n_ctx)
        return remote(
            part_send.at[peer],
            part_recv.at[k],
            part_send_sem.at[k],
            part_recv_sem.at[k],
            {"ctx": peer},
        )

    lax.fori_loop(1, n_ctx, start_of(partial), 0)
    summed = part_send[c].astype(f32)
    lax.fori_loop(1, n_ctx, wait_recv_of(partial), 0)
    for k in range(1, n_ctx):
        summed = summed + part_recv[k].astype(f32)
    gate = summed[:, :hidden_width]
    hidden_ref[c] = (gate / (1.0 + jnp.exp(-gate)) * summed[:, hidden_width:]).astype(bf16)

    def hidden_copy(k):
        return remote(
            hidden_ref.at[c],
            hidden_ref.at[c],
            hidden_send_sem.at[k],
            hidden_recv_sem.at[k],
            {"ctx": lax.rem(c + k, n_ctx)},
        )

    lax.fori_loop(1, n_ctx, start_of(hidden_copy), 0)
    loads[3].wait()
    lax.fori_loop(1, n_ctx, wait_recv_of(hidden_copy), 0)
    expert_out = jnp.dot(
        hidden_ref[...].reshape(-1, hidden_width), w_down[...], preferred_element_type=f32
    )
    back_send[...] = packed(expert_out)
    back = to_all(back_send, back_recv, back_send_sem, back_recv_sem)
    lax.fori_loop(1, devices, start_of(back), 0)
    back_recv[me] = back_send[me]
    lax.fori_loop(1, devices, wait_recv_of(back), 0)
    for block in range(n_ctx):
        rows = back_recv[block * n_exp : (block + 1) * n_exp].astype(f32)
        for p in range(pieces):
            begin = block * columns + p * piece
            mixed = jnp.dot(
                combine_ref[...],
                unpacked(rows, p),
                precision=lax.Precision.HIGHEST,
                preferred_element_type=f32,
            )
            out_ref[:, begin : begin + piece] = (
                residual[:, begin : begin + piece] + mixed
            ).astype(bf16)

    def sent_block(step, carry):
        @pl.when(jnp.logical_and(step <= c, c + 1 < n_ctx))
        def _():
            hop(kv_buf.at[c - step], c - step).wait_send()

        return carry

    lax.fori_loop(0, n_ctx, sent_block, 0)
    lax.fori_loop(1, n_exp, wait_send_of(share), 0)
    lax.fori_loop(1, devices, wait_send_of(dispatch), 0)
    lax.fori_loop(1, n_ctx, wait_send_of(partial), 0)
    lax.fori_loop(1, n_ctx, wait_send_of(hidden_copy), 0)
    lax.fori_loop(1, devices, wait_send_of(back), 0)


def body(
    tokens,
    positions,
    attn_gain,
    w_qkv,
    w_out,
    moe_gain,
    expert_ids,
    gate_probs,
    w_gate,
    w_up,
    w_down,
):
    seq_dev = tokens.shape[0]
    width = tokens.shape[1]
    head_dim = w_out.shape[1]
    heads_here = w_out.shape[0]
    n_ctx = lax.axis_size("ctx")
    n_exp = lax.axis_size("exp")
    devices = n_ctx * n_exp
    normed = rms_norm(tokens, attn_gain).astype(jnp.bfloat16)
    projected = jnp.einsum("sd,dhc->hsc", normed, w_qkv, preferred_element_type=jnp.float32)
    cosines, sines = rotary_tables(positions, head_dim)
    queries = rotate(projected[..., :head_dim], cosines, sines).astype(jnp.bfloat16)
    key_rows = rotate(projected[..., head_dim : 2 * head_dim], cosines, sines).astype(jnp.bfloat16)
    value_rows = projected[..., 2 * head_dim :].astype(jnp.bfloat16)
    keys_values = jnp.concatenate([key_rows, value_rows], axis=0)
    own = seq_dev // n_exp
    own_tokens = lax.dynamic_slice_in_dim(tokens, lax.axis_index("exp") * own, own, 0)

    flight = n_exp
    hits = expert_ids[:, :, None] == jnp.arange(flight, dtype=jnp.int32)[None, None, :]
    marks = jnp.any(hits, axis=1)
    weight = jnp.sum(jnp.where(hits, gate_probs[:, :, None], 0.0), axis=1)
    before = jnp.arange(own)[:, None] > jnp.arange(own)[None, :]
    place = jnp.sum((before[:, :, None] & marks[None, :, :]).astype(jnp.int32), axis=1)
    in_slot = marks[:, :, None] & (
        place[:, :, None] == jnp.arange(ROWS, dtype=jnp.int32)[None, None, :]
    )
    send_matrix = in_slot.reshape(own, flight * ROWS).T.astype(jnp.bfloat16)
    combine = jnp.where(in_slot, weight[:, :, None], 0.0).reshape(own, flight * ROWS)

    columns = width // n_ctx
    pieces = 2 if columns % 256 == 0 else 1
    piece = columns // pieces
    hidden_width = w_gate.shape[2]
    bf16 = jnp.bfloat16
    vmem = pl.BlockSpec(memory_space=pltpu.VMEM)
    anywhere = pl.BlockSpec(memory_space=pl.ANY)
    dma = pltpu.SemaphoreType.DMA
    return pl.pallas_call(
        functools.partial(layer_kernel, n_ctx, n_exp, pieces),
        out_shape=jax.ShapeDtypeStruct((own, width), bf16),
        in_specs=[vmem] * 6 + [anywhere] * 4,
        out_specs=vmem,
        scratch_shapes=[
            pltpu.VMEM((n_ctx, 2 * heads_here, seq_dev, head_dim), bf16),
            pltpu.VMEM((heads_here, seq_dev, 1), jnp.float32),
            pltpu.VMEM((heads_here, seq_dev, 1), jnp.float32),
            pltpu.VMEM((heads_here, seq_dev, head_dim), jnp.float32),
            pltpu.VMEM((seq_dev, heads_here * head_dim), bf16),
            pltpu.VMEM((heads_here * head_dim, width), bf16),
            pltpu.VMEM(w_gate.shape[1:], bf16),
            pltpu.VMEM(w_up.shape[1:], bf16),
            pltpu.VMEM(w_down.shape[1:], bf16),
            pltpu.VMEM((n_exp, own, width), bf16),
            pltpu.VMEM((n_exp, own, width), bf16),
            pltpu.VMEM((devices, 2 * ROWS, piece), bf16),
            pltpu.VMEM((devices, 2 * ROWS, piece), bf16),
            pltpu.VMEM((n_ctx, n_exp * ROWS, 2 * hidden_width), bf16),
            pltpu.VMEM((n_ctx, n_exp * ROWS, 2 * hidden_width), bf16),
            pltpu.VMEM((n_ctx, n_exp * ROWS, hidden_width), bf16),
            pltpu.VMEM((devices, 2 * ROWS, piece), bf16),
            pltpu.VMEM((devices, 2 * ROWS, piece), bf16),
            dma((4,)),
            dma((n_ctx,)),
            dma((n_ctx,)),
            dma((n_exp,)),
            dma((n_exp,)),
            dma((devices,)),
            dma((devices,)),
            dma((n_ctx,)),
            dma((n_ctx,)),
            dma((n_ctx,)),
            dma((n_ctx,)),
            dma((devices,)),
            dma((devices,)),
        ],
        compiler_params=pltpu.CompilerParams(
            collective_id=0, has_side_effects=True, vmem_limit_bytes=60 * 1024 * 1024
        ),
    )(
        queries,
        keys_values,
        own_tokens,
        moe_gain.reshape(1, width),
        send_matrix,
        combine,
        w_out.reshape(heads_here * head_dim, width),
        w_gate[0],
        w_up[0],
        w_down[0],
    )


def solution(mesh):
    return jax.shard_map(
        body,
        mesh=mesh,
        in_specs=(
            P(("groups", "ctx"), None),
            P(("groups", "ctx")),
            P(),
            P(None, "exp", None),
            P("exp", None, None),
            P(),
            P(("groups", "ctx", "exp"), None),
            P(("groups", "ctx", "exp"), None),
            P("exp", "ctx", None),
            P("exp", "ctx", None),
            P("exp", None, "ctx"),
        ),
        out_specs=P(("groups", "ctx", "exp"), None),
        check_vma=False,
    )
```

```python
import functools

import jax
import jax.numpy as jnp
from jax import lax
from jax.experimental import pallas as pl
from jax.experimental.pallas import tpu as pltpu
from jax.sharding import PartitionSpec as P

CAP = 6
ROWS = 8


epsilon = 1e-06


def rms_norm(rows, gain):
    rows = rows.astype(jnp.float32)
    return rows * lax.rsqrt(jnp.mean(rows * rows, axis=-1, keepdims=True) + epsilon) * gain


def rotary_tables(positions, width):
    freqs = 10000.0 ** (-jnp.arange(width // 2, dtype=jnp.float32) * 2.0 / width)
    angles = positions.astype(jnp.float32)[:, None] * freqs[None, :]
    cosines, sines = jnp.cos(angles), jnp.sin(angles)
    return (
        jnp.concatenate([cosines, cosines], axis=1),
        jnp.concatenate([-sines, sines], axis=1),
    )


def each(begin, end, step):
    if end - begin <= 16:
        for k in range(begin, end):
            step(k)
        return

    def one(k, carry):
        step(k)
        return carry

    lax.fori_loop(begin, end, one, 0)


def layer_kernel(
    n_ctx,
    n_exp,
    pieces,
    projected_ref,
    cosines_ref,
    sines_ref,
    tokens_ref,
    gain_ref,
    send_matrix_ref,
    combine_ref,
    w_out_hbm,
    w_gate_hbm,
    w_up_hbm,
    w_down_hbm,
    out_ref,
    q_ref,
    kv_buf,
    peak_ref,
    total_ref,
    sum_ref,
    attended_ref,
    w_out,
    w_gate,
    w_up,
    w_down,
    rs_send,
    rs_recv,
    rows_send,
    rows_recv,
    part_send,
    part_recv,
    hidden_ref,
    back_send,
    back_recv,
    weight_sem,
    kv_send_sem,
    kv_recv_sem,
    rs_send_sem,
    rs_recv_sem,
    rows_send_sem,
    rows_recv_sem,
    part_send_sem,
    part_recv_sem,
    hidden_send_sem,
    hidden_recv_sem,
    back_send_sem,
    back_recv_sem,
):
    f32 = jnp.float32
    bf16 = jnp.bfloat16
    devices = n_ctx * n_exp
    c = lax.axis_index("ctx")
    e = lax.axis_index("exp")
    me = c * n_exp + e
    heads, seq, head_dim = q_ref.shape
    width = tokens_ref.shape[1]
    own = seq // n_exp
    columns = width // n_ctx
    piece = columns // pieces
    hidden_width = w_gate.shape[1]

    loads = [
        pltpu.make_async_copy(w_out_hbm, w_out, weight_sem.at[0]),
        pltpu.make_async_copy(w_gate_hbm, w_gate, weight_sem.at[1]),
        pltpu.make_async_copy(w_up_hbm, w_up, weight_sem.at[2]),
        pltpu.make_async_copy(w_down_hbm, w_down, weight_sem.at[3]),
    ]
    for load in loads:
        load.start()

    barrier = pltpu.get_barrier_semaphore()

    def greet(k):
        peer = lax.rem(me + k, devices)
        pl.semaphore_signal(
            barrier,
            inc=1,
            device_id={"ctx": peer // n_exp, "exp": lax.rem(peer, n_exp)},
            device_id_type=pl.DeviceIdType.MESH,
        )

    each(1, devices, greet)

    def rotated(vectors):
        return (
            vectors * cosines_ref[...]
            + pltpu.roll(vectors, head_dim // 2, axis=1) * sines_ref[...]
        ).astype(bf16)

    for head in range(heads):
        kv_buf[c, head] = rotated(projected_ref[head, :, head_dim : 2 * head_dim])
        kv_buf[c, heads + head] = projected_ref[head, :, 2 * head_dim :].astype(bf16)
    pl.semaphore_wait(barrier, devices - 1)

    def remote(src, dst, send_sem, recv_sem, device):
        return pltpu.make_async_remote_copy(
            src_ref=src,
            dst_ref=dst,
            send_sem=send_sem,
            recv_sem=recv_sem,
            device_id=device,
            device_id_type=pl.DeviceIdType.MESH,
        )

    def hop(block):
        return remote(
            kv_buf.at[block],
            kv_buf.at[block],
            kv_send_sem.at[block],
            kv_recv_sem.at[block],
            {"ctx": lax.rem(c + 1, n_ctx)},
        )

    @pl.when(c + 1 < n_ctx)
    def _():
        hop(c).start()

    scale = head_dim ** (-0.5)
    over_last = (((1,), (1,)), ((), ()))
    allowed = lax.broadcasted_iota(jnp.int32, (seq, seq), 1) <= lax.broadcasted_iota(
        jnp.int32, (seq, seq), 0
    )
    for head in range(heads):
        q_ref[head] = rotated(projected_ref[head, :, :head_dim])
        scores = (
            lax.dot_general(q_ref[head], kv_buf[c, head], over_last, preferred_element_type=f32)
            * scale
        )
        scores = jnp.where(allowed, scores, -jnp.inf)
        peak = jnp.max(scores, axis=1, keepdims=True)
        probs = jnp.exp(scores - peak)
        peak_ref[head] = peak
        total_ref[head] = jnp.sum(probs, axis=1, keepdims=True)
        sum_ref[head] = jnp.dot(
            probs.astype(bf16), kv_buf[c, heads + head], preferred_element_type=f32
        )

    def earlier_block(step, carry):
        @pl.when(step <= c)
        def _():
            block = c - step
            hop(block).wait_recv()

            @pl.when(c + 1 < n_ctx)
            def _():
                hop(block).start()

            for head in range(heads):
                scores = (
                    lax.dot_general(
                        q_ref[head], kv_buf[block, head], over_last, preferred_element_type=f32
                    )
                    * scale
                )
                old_peak = peak_ref[head]
                peak = jnp.maximum(old_peak, jnp.max(scores, axis=1, keepdims=True))
                probs = jnp.exp(scores - peak)
                factor = jnp.exp(old_peak - peak)
                peak_ref[head] = peak
                total_ref[head] = total_ref[head] * factor + jnp.sum(probs, axis=1, keepdims=True)
                sum_ref[head] = sum_ref[head] * factor + jnp.dot(
                    probs.astype(bf16), kv_buf[block, heads + head], preferred_element_type=f32
                )

        return carry

    lax.fori_loop(1, n_ctx, earlier_block, 0)
    for head in range(heads):
        attended_ref[:, head * head_dim : (head + 1) * head_dim] = (
            sum_ref[head] / total_ref[head]
        ).astype(bf16)

    loads[0].wait()
    chunk = 512
    for start in range(0, width, chunk):
        part = jnp.dot(
            attended_ref[...], w_out[:, start : start + chunk], preferred_element_type=f32
        )
        rs_send[:, :, start : start + chunk] = part.astype(bf16).reshape(n_exp, own, chunk)

    def share(k):
        peer = lax.rem(e + k, n_exp)
        return remote(
            rs_send.at[peer],
            rs_recv.at[k],
            rs_send_sem.at[k],
            rs_recv_sem.at[k],
            {"exp": peer},
        )

    def start_of(copy_of):
        return lambda k: copy_of(k).start()

    def wait_recv_of(copy_of):
        return lambda k: copy_of(k).wait_recv()

    def wait_send_of(copy_of):
        return lambda k: copy_of(k).wait_send()

    each(1, n_exp, start_of(share))
    residual = tokens_ref[pl.ds(pl.multiple_of(e * own, own), own), :].astype(f32) + rs_send[e].astype(f32)
    each(1, n_exp, wait_recv_of(share))
    for k in range(1, n_exp):
        residual = residual + rs_recv[k].astype(f32)

    square = jnp.mean(residual * residual, axis=-1, keepdims=True)
    normed = (residual * lax.rsqrt(square + epsilon) * gain_ref[...]).astype(bf16)
    outgoing = jnp.dot(send_matrix_ref[...], normed, preferred_element_type=f32)

    def packed(rows):
        parts = [
            rows[:, p * piece : (p + 1) * piece].reshape(-1, ROWS, piece) for p in range(pieces)
        ]
        if pieces == 1:
            parts.append(jnp.zeros_like(parts[0]))
        return jnp.concatenate(parts, axis=1).astype(bf16)

    def unpacked(rows, p):
        return rows[:, p * ROWS : (p + 1) * ROWS, :].reshape(-1, piece)

    for block in range(n_ctx):
        rows_send[block * n_exp : (block + 1) * n_exp] = packed(
            outgoing[:, block * columns : (block + 1) * columns]
        )

    def to_all(send, recv, send_sem, recv_sem):
        def copy_of(k):
            peer = lax.rem(me + k, devices)
            return remote(
                send.at[peer],
                recv.at[me],
                send_sem.at[k],
                recv_sem.at[k],
                {"ctx": peer // n_exp, "exp": lax.rem(peer, n_exp)},
            )

        return copy_of

    dispatch = to_all(rows_send, rows_recv, rows_send_sem, rows_recv_sem)
    each(1, devices, start_of(dispatch))
    rows_recv[me] = rows_send[me]
    loads[1].wait()
    loads[2].wait()
    each(1, devices, wait_recv_of(dispatch))
    used = n_exp * CAP
    slot = lax.broadcasted_iota(jnp.int32, (used, n_exp * ROWS), 1)
    place = lax.rem(slot, ROWS)
    keep = jnp.logical_and(
        lax.broadcasted_iota(jnp.int32, slot.shape, 0) == (slot // ROWS) * CAP + place, place < CAP
    )
    keep = keep.astype(f32).astype(bf16)
    gate = None
    for p in range(pieces):
        rows = jnp.concatenate(
            [
                jnp.dot(
                    keep,
                    unpacked(
                        rows_recv[block * n_exp : (block + 1) * n_exp].astype(f32), p
                    ).astype(bf16),
                    preferred_element_type=f32,
                )
                for block in range(n_ctx)
            ],
            axis=0,
        ).astype(bf16)
        gate_p = jnp.dot(
            rows, w_gate[p * piece : (p + 1) * piece, :], preferred_element_type=f32
        )
        up_p = jnp.dot(rows, w_up[p * piece : (p + 1) * piece, :], preferred_element_type=f32)
        gate, up = (gate_p, up_p) if gate is None else (gate + gate_p, up + up_p)
    for block in range(n_ctx):
        mine = slice(block * used, (block + 1) * used)
        part_send[block] = jnp.concatenate([gate[mine], up[mine]], axis=0).astype(bf16)

    def partial(k):
        peer = lax.rem(c + k, n_ctx)
        return remote(
            part_send.at[peer],
            part_recv.at[k],
            part_send_sem.at[k],
            part_recv_sem.at[k],
            {"ctx": peer},
        )

    each(1, n_ctx, start_of(partial))
    summed = part_send[c].astype(f32)
    each(1, n_ctx, wait_recv_of(partial))
    for k in range(1, n_ctx):
        summed = summed + part_recv[k].astype(f32)
    gate = summed[:used]
    hidden = gate / (1.0 + jnp.exp(-gate)) * summed[used:]
    half = hidden_width // 2
    hidden_ref[c] = jnp.concatenate([hidden[:, :half], hidden[:, half:]], axis=0).astype(bf16)

    def hidden_copy(k):
        return remote(
            hidden_ref.at[c],
            hidden_ref.at[c],
            hidden_send_sem.at[k],
            hidden_recv_sem.at[k],
            {"ctx": lax.rem(c + k, n_ctx)},
        )

    each(1, n_ctx, start_of(hidden_copy))
    loads[3].wait()
    each(1, n_ctx, wait_recv_of(hidden_copy))
    hidden = hidden_ref[...].astype(f32)
    expert_out = None
    for p in range(2):
        rows = hidden[:, p * used : (p + 1) * used, :].reshape(-1, half).astype(bf16)
        out_p = jnp.dot(rows, w_down[p * half : (p + 1) * half, :], preferred_element_type=f32)
        expert_out = out_p if expert_out is None else expert_out + out_p
    for block in range(n_ctx):
        rows = expert_out[block * used : (block + 1) * used].astype(bf16)
        rows = lax.dot_general(keep, rows, (((0,), (0,)), ((), ())), preferred_element_type=f32)
        back_send[block * n_exp : (block + 1) * n_exp] = packed(rows)
    back = to_all(back_send, back_recv, back_send_sem, back_recv_sem)
    each(1, devices, start_of(back))
    back_recv[me] = back_send[me]
    each(1, devices, wait_recv_of(back))
    for block in range(n_ctx):
        rows = back_recv[block * n_exp : (block + 1) * n_exp].astype(f32)
        for p in range(pieces):
            begin = block * columns + p * piece
            mixed = jnp.dot(
                combine_ref[...],
                unpacked(rows, p),
                precision=lax.Precision.HIGHEST,
                preferred_element_type=f32,
            )
            out_ref[:, begin : begin + piece] = (
                residual[:, begin : begin + piece] + mixed
            ).astype(bf16)

    def sent_block(step, carry):
        @pl.when(jnp.logical_and(step <= c, c + 1 < n_ctx))
        def _():
            hop(c - step).wait_send()

        return carry

    lax.fori_loop(0, n_ctx, sent_block, 0)
    each(1, n_exp, wait_send_of(share))
    each(1, devices, wait_send_of(dispatch))
    each(1, n_ctx, wait_send_of(partial))
    each(1, n_ctx, wait_send_of(hidden_copy))
    each(1, devices, wait_send_of(back))


def body(
    tokens,
    positions,
    attn_gain,
    w_qkv,
    w_out,
    moe_gain,
    expert_ids,
    gate_probs,
    w_gate,
    w_up,
    w_down,
):
    seq_dev = tokens.shape[0]
    width = tokens.shape[1]
    head_dim = w_out.shape[1]
    heads_here = w_out.shape[0]
    n_ctx = lax.axis_size("ctx")
    n_exp = lax.axis_size("exp")
    devices = n_ctx * n_exp
    normed = rms_norm(tokens, attn_gain).astype(jnp.bfloat16)
    projected = jnp.einsum("sd,dhc->hsc", normed, w_qkv, preferred_element_type=jnp.float32)
    cosines, sines = rotary_tables(positions, head_dim)
    own = seq_dev // n_exp

    flight = n_exp
    hits = expert_ids[:, :, None] == jnp.arange(flight, dtype=jnp.int32)[None, None, :]
    marks = jnp.any(hits, axis=1)
    weight = jnp.sum(jnp.where(hits, gate_probs[:, :, None], 0.0), axis=1)
    before = jnp.arange(own)[:, None] > jnp.arange(own)[None, :]
    place = jnp.sum((before[:, :, None] & marks[None, :, :]).astype(jnp.int32), axis=1)
    in_slot = marks[:, :, None] & (
        place[:, :, None] == jnp.arange(ROWS, dtype=jnp.int32)[None, None, :]
    )
    send_matrix = in_slot.reshape(own, flight * ROWS).T.astype(jnp.bfloat16)
    combine = jnp.where(in_slot, weight[:, :, None], 0.0).reshape(own, flight * ROWS)

    columns = width // n_ctx
    pieces = 2 if columns % 256 == 0 else 1
    piece = columns // pieces
    hidden_width = w_gate.shape[2]
    bf16 = jnp.bfloat16
    vmem = pl.BlockSpec(memory_space=pltpu.VMEM)
    anywhere = pl.BlockSpec(memory_space=pl.ANY)
    dma = pltpu.SemaphoreType.DMA
    return pl.pallas_call(
        functools.partial(layer_kernel, n_ctx, n_exp, pieces),
        out_shape=jax.ShapeDtypeStruct((own, width), bf16),
        in_specs=[vmem] * 7 + [anywhere] * 4,
        out_specs=vmem,
        scratch_shapes=[
            pltpu.VMEM((heads_here, seq_dev, head_dim), bf16),
            pltpu.VMEM((n_ctx, 2 * heads_here, seq_dev, head_dim), bf16),
            pltpu.VMEM((heads_here, seq_dev, 1), jnp.float32),
            pltpu.VMEM((heads_here, seq_dev, 1), jnp.float32),
            pltpu.VMEM((heads_here, seq_dev, head_dim), jnp.float32),
            pltpu.VMEM((seq_dev, heads_here * head_dim), bf16),
            pltpu.VMEM((heads_here * head_dim, width), bf16),
            pltpu.VMEM(w_gate.shape[1:], bf16),
            pltpu.VMEM(w_up.shape[1:], bf16),
            pltpu.VMEM(w_down.shape[1:], bf16),
            pltpu.VMEM((n_exp, own, width), bf16),
            pltpu.VMEM((n_exp, own, width), bf16),
            pltpu.VMEM((devices, 2 * ROWS, piece), bf16),
            pltpu.VMEM((devices, 2 * ROWS, piece), bf16),
            pltpu.VMEM((n_ctx, 2 * n_exp * CAP, hidden_width), bf16),
            pltpu.VMEM((n_ctx, 2 * n_exp * CAP, hidden_width), bf16),
            pltpu.VMEM((n_ctx, 2 * n_exp * CAP, hidden_width // 2), bf16),
            pltpu.VMEM((devices, 2 * ROWS, piece), bf16),
            pltpu.VMEM((devices, 2 * ROWS, piece), bf16),
            dma((4,)),
            dma((n_ctx,)),
            dma((n_ctx,)),
            dma((n_exp,)),
            dma((n_exp,)),
            dma((devices,)),
            dma((devices,)),
            dma((n_ctx,)),
            dma((n_ctx,)),
            dma((n_ctx,)),
            dma((n_ctx,)),
            dma((devices,)),
            dma((devices,)),
        ],
        compiler_params=pltpu.CompilerParams(
            collective_id=0, has_side_effects=True, vmem_limit_bytes=60 * 1024 * 1024
        ),
    )(
        projected,
        cosines,
        sines,
        tokens,
        moe_gain.reshape(1, width),
        send_matrix,
        combine,
        w_out.reshape(heads_here * head_dim, width),
        w_gate[0],
        w_up[0],
        w_down[0],
    )


def solution(mesh):
    return jax.shard_map(
        body,
        mesh=mesh,
        in_specs=(
            P(("groups", "ctx"), None),
            P(("groups", "ctx")),
            P(),
            P(None, "exp", None),
            P("exp", None, None),
            P(),
            P(("groups", "ctx", "exp"), None),
            P(("groups", "ctx", "exp"), None),
            P("exp", "ctx", None),
            P("exp", "ctx", None),
            P("exp", None, "ctx"),
        ),
        out_specs=P(("groups", "ctx", "exp"), None),
        check_vma=False,
    )
```

```python
import functools

import jax
import jax.numpy as jnp
from jax import lax
from jax.experimental import pallas as pl
from jax.experimental.pallas import tpu as pltpu
from jax.sharding import PartitionSpec as P

CAP = 6
ROWS = 8


epsilon = 1e-06


def rms_norm(rows, gain):
    rows = rows.astype(jnp.float32)
    return rows * lax.rsqrt(jnp.mean(rows * rows, axis=-1, keepdims=True) + epsilon) * gain


def rotary_tables(positions, width):
    freqs = 10000.0 ** (-jnp.arange(width // 2, dtype=jnp.float32) * 2.0 / width)
    angles = positions.astype(jnp.float32)[:, None] * freqs[None, :]
    cosines, sines = jnp.cos(angles), jnp.sin(angles)
    return (
        jnp.concatenate([cosines, cosines], axis=1),
        jnp.concatenate([-sines, sines], axis=1),
    )


def each(begin, end, step):
    if end - begin <= 16:
        for k in range(begin, end):
            step(k)
        return

    def one(k, carry):
        step(k)
        return carry

    lax.fori_loop(begin, end, one, 0)


def layer_kernel(
    n_ctx,
    n_exp,
    pieces,
    groups,
    projected_ref,
    cosines_ref,
    sines_ref,
    tokens_ref,
    gain_ref,
    ids_ref,
    probs_ref,
    w_out_hbm,
    w_gate_hbm,
    w_up_hbm,
    w_down_hbm,
    out_ref,
    combine_ref,
    q_ref,
    kv_buf,
    peak_ref,
    total_ref,
    sum_ref,
    attended_ref,
    w_out,
    w_gate,
    w_up,
    w_down,
    rs_send,
    rs_recv,
    rows_send,
    rows_recv,
    part_send,
    part_recv,
    hidden_ref,
    back_send,
    back_recv,
    weight_sem,
    kv_send_sem,
    kv_recv_sem,
    rs_send_sem,
    rs_recv_sem,
    rows_send_sem,
    rows_recv_sem,
    part_send_sem,
    part_recv_sem,
    hidden_send_sem,
    hidden_recv_sem,
    back_send_sem,
    back_recv_sem,
):
    f32 = jnp.float32
    bf16 = jnp.bfloat16
    devices = n_ctx * n_exp
    c = lax.axis_index("ctx")
    e = lax.axis_index("exp")
    me = c * n_exp + e
    heads, seq, head_dim = q_ref.shape
    width = tokens_ref.shape[1]
    own = seq // n_exp
    columns = width // n_ctx
    piece = columns // pieces
    hidden_width = w_gate.shape[1]

    loads = [
        pltpu.make_async_copy(w_out_hbm, w_out, weight_sem.at[0]),
        pltpu.make_async_copy(w_gate_hbm, w_gate, weight_sem.at[1]),
        pltpu.make_async_copy(w_up_hbm, w_up, weight_sem.at[2]),
        pltpu.make_async_copy(w_down_hbm, w_down, weight_sem.at[3]),
    ]
    for load in loads:
        load.start()

    barrier = pltpu.get_barrier_semaphore()

    def greet(k):
        peer = lax.rem(me + k, devices)
        pl.semaphore_signal(
            barrier,
            inc=1,
            device_id={"ctx": peer // n_exp, "exp": lax.rem(peer, n_exp)},
            device_id_type=pl.DeviceIdType.MESH,
        )

    each(1, devices, greet)

    def rotated(vectors):
        return (
            vectors * cosines_ref[...]
            + pltpu.roll(vectors, head_dim // 2, axis=1) * sines_ref[...]
        ).astype(bf16)

    def remote(src, dst, send_sem, recv_sem, device):
        return pltpu.make_async_remote_copy(
            src_ref=src,
            dst_ref=dst,
            send_sem=send_sem,
            recv_sem=recv_sem,
            device_id=device,
            device_id_type=pl.DeviceIdType.MESH,
        )

    group = heads // groups

    def hop(block, part):
        heads_of = pl.ds(part * 2 * group, 2 * group)
        return remote(
            kv_buf.at[block, heads_of],
            kv_buf.at[block, heads_of],
            kv_send_sem.at[block, part],
            kv_recv_sem.at[block, part],
            {"ctx": lax.rem(c + 1, n_ctx)},
        )

    for part in range(groups):
        for head in range(part * group, (part + 1) * group):
            kv_buf[c, 2 * head] = rotated(projected_ref[head, :, head_dim : 2 * head_dim])
            kv_buf[c, 2 * head + 1] = projected_ref[head, :, 2 * head_dim :].astype(bf16)
        if part == 0:
            pl.semaphore_wait(barrier, devices - 1)

        @pl.when(c + 1 < n_ctx)
        def _():
            hop(c, part).start()

    scale = head_dim ** (-0.5)
    over_last = (((1,), (1,)), ((), ()))
    allowed = lax.broadcasted_iota(jnp.int32, (seq, seq), 1) <= lax.broadcasted_iota(
        jnp.int32, (seq, seq), 0
    )
    for head in range(heads):
        q_ref[head] = rotated(projected_ref[head, :, :head_dim])
        scores = (
            lax.dot_general(q_ref[head], kv_buf[c, 2 * head], over_last, preferred_element_type=f32)
            * scale
        )
        scores = jnp.where(allowed, scores, -jnp.inf)
        peak = jnp.max(scores, axis=1, keepdims=True)
        probs = jnp.exp(scores - peak)
        peak_ref[head] = peak
        total_ref[head] = jnp.sum(probs, axis=1, keepdims=True)
        sum_ref[head] = jnp.dot(
            probs.astype(bf16), kv_buf[c, 2 * head + 1], preferred_element_type=f32
        )

    slots = n_exp * ROWS
    slot_of = lax.broadcasted_iota(jnp.int32, (own, slots), 1)
    marks = jnp.zeros((own, slots), f32)
    weight = jnp.zeros((own, slots), f32)
    for k in range(ids_ref.shape[1]):
        hit = ids_ref[:, k : k + 1] == slot_of // ROWS
        marks = jnp.where(hit, 1.0, marks)
        weight = weight + jnp.where(hit, probs_ref[:, k : k + 1], 0.0)
    before = lax.broadcasted_iota(jnp.int32, (own, own), 1) < lax.broadcasted_iota(
        jnp.int32, (own, own), 0
    )
    place = jnp.dot(
        before.astype(f32).astype(bf16), marks.astype(bf16), preferred_element_type=f32
    )
    in_slot = jnp.where(place == lax.rem(slot_of, ROWS).astype(f32), marks, 0.0)
    combine_ref[...] = in_slot * weight
    in_slot = in_slot.astype(bf16)

    def earlier_block(step, carry):
        @pl.when(step <= c)
        def _():
            block = c - step
            for part in range(groups):
                hop(block, part).wait_recv()

                @pl.when(c + 1 < n_ctx)
                def _():
                    hop(block, part).start()

                for head in range(part * group, (part + 1) * group):
                    scores = (
                        lax.dot_general(
                            q_ref[head],
                            kv_buf[block, 2 * head],
                            over_last,
                            preferred_element_type=f32,
                        )
                        * scale
                    )
                    old_peak = peak_ref[head]
                    peak = jnp.maximum(old_peak, jnp.max(scores, axis=1, keepdims=True))
                    probs = jnp.exp(scores - peak)
                    factor = jnp.exp(old_peak - peak)
                    peak_ref[head] = peak
                    total_ref[head] = total_ref[head] * factor + jnp.sum(
                        probs, axis=1, keepdims=True
                    )
                    sum_ref[head] = sum_ref[head] * factor + jnp.dot(
                        probs.astype(bf16),
                        kv_buf[block, 2 * head + 1],
                        preferred_element_type=f32,
                    )

        return carry

    lax.fori_loop(1, n_ctx, earlier_block, 0)
    for head in range(heads):
        attended_ref[:, head * head_dim : (head + 1) * head_dim] = (
            sum_ref[head] / total_ref[head]
        ).astype(bf16)

    loads[0].wait()
    chunk = 512
    for start in range(0, width, chunk):
        part = jnp.dot(
            attended_ref[...], w_out[:, start : start + chunk], preferred_element_type=f32
        )
        rs_send[:, :, start : start + chunk] = part.astype(bf16).reshape(n_exp, own, chunk)

    def share(k):
        peer = lax.rem(e + k, n_exp)
        return remote(
            rs_send.at[peer],
            rs_recv.at[k],
            rs_send_sem.at[k],
            rs_recv_sem.at[k],
            {"exp": peer},
        )

    def start_of(copy_of):
        return lambda k: copy_of(k).start()

    def wait_recv_of(copy_of):
        return lambda k: copy_of(k).wait_recv()

    def wait_send_of(copy_of):
        return lambda k: copy_of(k).wait_send()

    each(1, n_exp, start_of(share))
    residual = tokens_ref[pl.ds(pl.multiple_of(e * own, own), own), :].astype(f32) + rs_send[e].astype(f32)
    each(1, n_exp, wait_recv_of(share))
    for k in range(1, n_exp):
        residual = residual + rs_recv[k].astype(f32)

    square = jnp.mean(residual * residual, axis=-1, keepdims=True)
    normed = (residual * lax.rsqrt(square + epsilon) * gain_ref[...]).astype(bf16)
    outgoing = lax.dot_general(
        in_slot, normed, (((0,), (0,)), ((), ())), preferred_element_type=f32
    )

    def packed(rows):
        parts = [
            rows[:, p * piece : (p + 1) * piece].reshape(-1, ROWS, piece) for p in range(pieces)
        ]
        if pieces == 1:
            parts.append(jnp.zeros_like(parts[0]))
        return jnp.concatenate(parts, axis=1).astype(bf16)

    def unpacked(rows, p):
        return rows[:, p * ROWS : (p + 1) * ROWS, :].reshape(-1, piece)

    for block in range(n_ctx):
        rows_send[block * n_exp : (block + 1) * n_exp] = packed(
            outgoing[:, block * columns : (block + 1) * columns]
        )

    def to_all(send, recv, send_sem, recv_sem):
        def copy_of(k):
            peer = lax.rem(me + k, devices)
            return remote(
                send.at[peer],
                recv.at[me],
                send_sem.at[k],
                recv_sem.at[k],
                {"ctx": peer // n_exp, "exp": lax.rem(peer, n_exp)},
            )

        return copy_of

    dispatch = to_all(rows_send, rows_recv, rows_send_sem, rows_recv_sem)
    each(1, devices, start_of(dispatch))
    rows_recv[me] = rows_send[me]
    loads[1].wait()
    loads[2].wait()
    each(1, devices, wait_recv_of(dispatch))
    used = n_exp * CAP
    slot = lax.broadcasted_iota(jnp.int32, (used, n_exp * ROWS), 1)
    place = lax.rem(slot, ROWS)
    keep = jnp.logical_and(
        lax.broadcasted_iota(jnp.int32, slot.shape, 0) == (slot // ROWS) * CAP + place, place < CAP
    )
    keep = keep.astype(f32).astype(bf16)
    gate = None
    for p in range(pieces):
        rows = jnp.concatenate(
            [
                jnp.dot(
                    keep,
                    unpacked(
                        rows_recv[block * n_exp : (block + 1) * n_exp].astype(f32), p
                    ).astype(bf16),
                    preferred_element_type=f32,
                )
                for block in range(n_ctx)
            ],
            axis=0,
        ).astype(bf16)
        gate_p = jnp.dot(
            rows, w_gate[p * piece : (p + 1) * piece, :], preferred_element_type=f32
        )
        up_p = jnp.dot(rows, w_up[p * piece : (p + 1) * piece, :], preferred_element_type=f32)
        gate, up = (gate_p, up_p) if gate is None else (gate + gate_p, up + up_p)
    for block in range(n_ctx):
        mine = slice(block * used, (block + 1) * used)
        part_send[block] = jnp.concatenate([gate[mine], up[mine]], axis=0).astype(bf16)

    def partial(k):
        peer = lax.rem(c + k, n_ctx)
        return remote(
            part_send.at[peer],
            part_recv.at[k],
            part_send_sem.at[k],
            part_recv_sem.at[k],
            {"ctx": peer},
        )

    each(1, n_ctx, start_of(partial))
    summed = part_send[c].astype(f32)
    each(1, n_ctx, wait_recv_of(partial))
    for k in range(1, n_ctx):
        summed = summed + part_recv[k].astype(f32)
    gate = summed[:used]
    hidden = gate / (1.0 + jnp.exp(-gate)) * summed[used:]
    half = hidden_width // 2
    hidden_ref[c] = jnp.concatenate([hidden[:, :half], hidden[:, half:]], axis=0).astype(bf16)

    def hidden_copy(k):
        return remote(
            hidden_ref.at[c],
            hidden_ref.at[c],
            hidden_send_sem.at[k],
            hidden_recv_sem.at[k],
            {"ctx": lax.rem(c + k, n_ctx)},
        )

    each(1, n_ctx, start_of(hidden_copy))
    loads[3].wait()
    each(1, n_ctx, wait_recv_of(hidden_copy))
    hidden = hidden_ref[...].astype(f32)
    expert_out = None
    for p in range(2):
        rows = hidden[:, p * used : (p + 1) * used, :].reshape(-1, half).astype(bf16)
        out_p = jnp.dot(rows, w_down[p * half : (p + 1) * half, :], preferred_element_type=f32)
        expert_out = out_p if expert_out is None else expert_out + out_p
    for block in range(n_ctx):
        rows = expert_out[block * used : (block + 1) * used].astype(bf16)
        rows = lax.dot_general(keep, rows, (((0,), (0,)), ((), ())), preferred_element_type=f32)
        back_send[block * n_exp : (block + 1) * n_exp] = packed(rows)
    back = to_all(back_send, back_recv, back_send_sem, back_recv_sem)
    each(1, devices, start_of(back))
    back_recv[me] = back_send[me]
    each(1, devices, wait_recv_of(back))
    for block in range(n_ctx):
        rows = back_recv[block * n_exp : (block + 1) * n_exp].astype(f32)
        for p in range(pieces):
            begin = block * columns + p * piece
            mixed = jnp.dot(
                combine_ref[...],
                unpacked(rows, p),
                precision=lax.Precision.HIGHEST,
                preferred_element_type=f32,
            )
            out_ref[:, begin : begin + piece] = (
                residual[:, begin : begin + piece] + mixed
            ).astype(bf16)

    def sent_block(step, carry):
        @pl.when(jnp.logical_and(step <= c, c + 1 < n_ctx))
        def _():
            for part in range(groups):
                hop(c - step, part).wait_send()

        return carry

    lax.fori_loop(0, n_ctx, sent_block, 0)
    each(1, n_exp, wait_send_of(share))
    each(1, devices, wait_send_of(dispatch))
    each(1, n_ctx, wait_send_of(partial))
    each(1, n_ctx, wait_send_of(hidden_copy))
    each(1, devices, wait_send_of(back))


def body(
    tokens,
    positions,
    attn_gain,
    w_qkv,
    w_out,
    moe_gain,
    expert_ids,
    gate_probs,
    w_gate,
    w_up,
    w_down,
):
    seq_dev = tokens.shape[0]
    width = tokens.shape[1]
    head_dim = w_out.shape[1]
    heads_here = w_out.shape[0]
    n_ctx = lax.axis_size("ctx")
    n_exp = lax.axis_size("exp")
    devices = n_ctx * n_exp
    normed = rms_norm(tokens, attn_gain).astype(jnp.bfloat16)
    projected = jnp.einsum("sd,dhc->hsc", normed, w_qkv, preferred_element_type=jnp.float32)
    cosines, sines = rotary_tables(positions, head_dim)
    own = seq_dev // n_exp

    columns = width // n_ctx
    pieces = 2 if columns % 256 == 0 else 1
    piece = columns // pieces
    groups = heads_here
    hidden_width = w_gate.shape[2]
    bf16 = jnp.bfloat16
    vmem = pl.BlockSpec(memory_space=pltpu.VMEM)
    anywhere = pl.BlockSpec(memory_space=pl.ANY)
    dma = pltpu.SemaphoreType.DMA
    return pl.pallas_call(
        functools.partial(layer_kernel, n_ctx, n_exp, pieces, groups),
        out_shape=jax.ShapeDtypeStruct((own, width), bf16),
        in_specs=[vmem] * 7 + [anywhere] * 4,
        out_specs=vmem,
        scratch_shapes=[
            pltpu.VMEM((own, n_exp * ROWS), jnp.float32),
            pltpu.VMEM((heads_here, seq_dev, head_dim), bf16),
            pltpu.VMEM((n_ctx, 2 * heads_here, seq_dev, head_dim), bf16),
            pltpu.VMEM((heads_here, seq_dev, 1), jnp.float32),
            pltpu.VMEM((heads_here, seq_dev, 1), jnp.float32),
            pltpu.VMEM((heads_here, seq_dev, head_dim), jnp.float32),
            pltpu.VMEM((seq_dev, heads_here * head_dim), bf16),
            pltpu.VMEM((heads_here * head_dim, width), bf16),
            pltpu.VMEM(w_gate.shape[1:], bf16),
            pltpu.VMEM(w_up.shape[1:], bf16),
            pltpu.VMEM(w_down.shape[1:], bf16),
            pltpu.VMEM((n_exp, own, width), bf16),
            pltpu.VMEM((n_exp, own, width), bf16),
            pltpu.VMEM((devices, 2 * ROWS, piece), bf16),
            pltpu.VMEM((devices, 2 * ROWS, piece), bf16),
            pltpu.VMEM((n_ctx, 2 * n_exp * CAP, hidden_width), bf16),
            pltpu.VMEM((n_ctx, 2 * n_exp * CAP, hidden_width), bf16),
            pltpu.VMEM((n_ctx, 2 * n_exp * CAP, hidden_width // 2), bf16),
            pltpu.VMEM((devices, 2 * ROWS, piece), bf16),
            pltpu.VMEM((devices, 2 * ROWS, piece), bf16),
            dma((4,)),
            dma((n_ctx, groups)),
            dma((n_ctx, groups)),
            dma((n_exp,)),
            dma((n_exp,)),
            dma((devices,)),
            dma((devices,)),
            dma((n_ctx,)),
            dma((n_ctx,)),
            dma((n_ctx,)),
            dma((n_ctx,)),
            dma((devices,)),
            dma((devices,)),
        ],
        compiler_params=pltpu.CompilerParams(
            collective_id=0, has_side_effects=True, vmem_limit_bytes=60 * 1024 * 1024
        ),
    )(
        projected,
        cosines,
        sines,
        tokens,
        moe_gain.reshape(1, width),
        expert_ids,
        gate_probs,
        w_out.reshape(heads_here * head_dim, width),
        w_gate[0],
        w_up[0],
        w_down[0],
    )


def solution(mesh):
    return jax.shard_map(
        body,
        mesh=mesh,
        in_specs=(
            P(("groups", "ctx"), None),
            P(("groups", "ctx")),
            P(),
            P(None, "exp", None),
            P("exp", None, None),
            P(),
            P(("groups", "ctx", "exp"), None),
            P(("groups", "ctx", "exp"), None),
            P("exp", "ctx", None),
            P("exp", "ctx", None),
            P("exp", None, "ctx"),
        ),
        out_specs=P(("groups", "ctx", "exp"), None),
        check_vma=False,
    )
```

```python
import functools

import jax
import jax.numpy as jnp
from jax import lax
from jax.experimental import pallas as pl
from jax.experimental.pallas import tpu as pltpu
from jax.sharding import PartitionSpec as P

CAP = 6
ROWS = 8


epsilon = 1e-06


def rms_norm(rows, gain):
    rows = rows.astype(jnp.float32)
    return rows * lax.rsqrt(jnp.mean(rows * rows, axis=-1, keepdims=True) + epsilon) * gain


def rotary_tables(positions, width):
    half = width // 2
    column = jnp.arange(width, dtype=jnp.int32)
    freqs = 10000.0 ** (-(column % half).astype(jnp.float32) * 2.0 / width)
    angles = positions.astype(jnp.float32)[:, None] * freqs[None, :]
    return (jnp.cos(angles), jnp.where(column < half, -1.0, 1.0)[None, :] * jnp.sin(angles))


def each(begin, end, step):
    if end - begin <= 16:
        for k in range(begin, end):
            step(k)
        return

    def one(k, carry):
        step(k)
        return carry

    lax.fori_loop(begin, end, one, 0)


def layer_kernel(
    n_ctx,
    n_exp,
    pieces,
    groups,
    projected_ref,
    cosines_ref,
    sines_ref,
    tokens_ref,
    gain_ref,
    ids_ref,
    probs_ref,
    w_out_hbm,
    w_gate_hbm,
    w_up_hbm,
    w_down_hbm,
    out_ref,
    combine_ref,
    q_ref,
    kv_buf,
    peak_ref,
    total_ref,
    sum_ref,
    attended_ref,
    w_out,
    w_gate,
    w_up,
    w_down,
    rs_send,
    rs_recv,
    rows_send,
    rows_recv,
    part_send,
    part_recv,
    hidden_ref,
    back_send,
    back_recv,
    weight_sem,
    kv_send_sem,
    kv_recv_sem,
    rs_send_sem,
    rs_recv_sem,
    rows_send_sem,
    rows_recv_sem,
    part_send_sem,
    part_recv_sem,
    hidden_send_sem,
    hidden_recv_sem,
    back_send_sem,
    back_recv_sem,
):
    f32 = jnp.float32
    bf16 = jnp.bfloat16
    devices = n_ctx * n_exp
    c = lax.axis_index("ctx")
    e = lax.axis_index("exp")
    me = c * n_exp + e
    heads, seq, head_dim = q_ref.shape
    width = tokens_ref.shape[1]
    own = seq // n_exp
    columns = width // n_ctx
    piece = columns // pieces
    hidden_width = w_gate.shape[1]

    loads = [
        pltpu.make_async_copy(w_out_hbm, w_out, weight_sem.at[0]),
        pltpu.make_async_copy(w_gate_hbm, w_gate, weight_sem.at[1]),
        pltpu.make_async_copy(w_up_hbm, w_up, weight_sem.at[2]),
        pltpu.make_async_copy(w_down_hbm, w_down, weight_sem.at[3]),
    ]
    for load in loads:
        load.start()

    barrier = pltpu.get_barrier_semaphore()

    def greet(k):
        peer = lax.rem(me + k, devices)
        pl.semaphore_signal(
            barrier,
            inc=1,
            device_id={"ctx": peer // n_exp, "exp": lax.rem(peer, n_exp)},
            device_id_type=pl.DeviceIdType.MESH,
        )

    each(1, devices, greet)

    def rotated(vectors):
        return (
            vectors * cosines_ref[...]
            + pltpu.roll(vectors, head_dim // 2, axis=1) * sines_ref[...]
        ).astype(bf16)

    def remote(src, dst, send_sem, recv_sem, device):
        return pltpu.make_async_remote_copy(
            src_ref=src,
            dst_ref=dst,
            send_sem=send_sem,
            recv_sem=recv_sem,
            device_id=device,
            device_id_type=pl.DeviceIdType.MESH,
        )

    group = heads // groups

    def hop(block, part):
        heads_of = pl.ds(part * 2 * group, 2 * group)
        return remote(
            kv_buf.at[block, heads_of],
            kv_buf.at[block, heads_of],
            kv_send_sem.at[block, part],
            kv_recv_sem.at[block, part],
            {"ctx": lax.rem(c + 1, n_ctx)},
        )

    for part in range(groups):
        for head in range(part * group, (part + 1) * group):
            kv_buf[c, 2 * head] = rotated(projected_ref[head, :, head_dim : 2 * head_dim])
            kv_buf[c, 2 * head + 1] = projected_ref[head, :, 2 * head_dim :].astype(bf16)
        if part == 0:
            pl.semaphore_wait(barrier, devices - 1)

        @pl.when(c + 1 < n_ctx)
        def _():
            hop(c, part).start()

    scale = head_dim ** (-0.5)
    over_last = (((1,), (1,)), ((), ()))
    allowed = lax.broadcasted_iota(jnp.int32, (seq, seq), 1) <= lax.broadcasted_iota(
        jnp.int32, (seq, seq), 0
    )
    for head in range(heads):
        q_ref[head] = rotated(projected_ref[head, :, :head_dim])
        scores = (
            lax.dot_general(q_ref[head], kv_buf[c, 2 * head], over_last, preferred_element_type=f32)
            * scale
        )
        scores = jnp.where(allowed, scores, -jnp.inf)
        peak = jnp.max(scores, axis=1, keepdims=True)
        probs = jnp.exp(scores - peak)
        peak_ref[head] = peak
        total_ref[head] = jnp.sum(probs, axis=1, keepdims=True)
        sum_ref[head] = jnp.dot(
            probs.astype(bf16), kv_buf[c, 2 * head + 1], preferred_element_type=f32
        )

    slots = n_exp * ROWS
    slot_of = lax.broadcasted_iota(jnp.int32, (slots, own), 0)
    marks = jnp.zeros((slots, own), f32)
    weight = jnp.zeros((slots, own), f32)
    for k in range(ids_ref.shape[0]):
        hit = ids_ref[k : k + 1, :] == slot_of // ROWS
        marks = jnp.where(hit, 1.0, marks)
        weight = weight + jnp.where(hit, probs_ref[k : k + 1, :], 0.0)
    before = lax.broadcasted_iota(jnp.int32, (own, own), 0) < lax.broadcasted_iota(
        jnp.int32, (own, own), 1
    )
    place = jnp.dot(
        marks.astype(bf16), before.astype(f32).astype(bf16), preferred_element_type=f32
    )
    in_slot = jnp.where(place == lax.rem(slot_of, ROWS).astype(f32), marks, 0.0)
    combine_ref[...] = (in_slot * weight).T
    in_slot = in_slot.astype(bf16)

    def earlier_block(step, carry):
        @pl.when(step <= c)
        def _():
            block = c - step
            for part in range(groups):
                hop(block, part).wait_recv()

                @pl.when(c + 1 < n_ctx)
                def _():
                    hop(block, part).start()

                for head in range(part * group, (part + 1) * group):
                    scores = (
                        lax.dot_general(
                            q_ref[head],
                            kv_buf[block, 2 * head],
                            over_last,
                            preferred_element_type=f32,
                        )
                        * scale
                    )
                    old_peak = peak_ref[head]
                    peak = jnp.maximum(old_peak, jnp.max(scores, axis=1, keepdims=True))
                    probs = jnp.exp(scores - peak)
                    factor = jnp.exp(old_peak - peak)
                    peak_ref[head] = peak
                    total_ref[head] = total_ref[head] * factor + jnp.sum(
                        probs, axis=1, keepdims=True
                    )
                    sum_ref[head] = sum_ref[head] * factor + jnp.dot(
                        probs.astype(bf16),
                        kv_buf[block, 2 * head + 1],
                        preferred_element_type=f32,
                    )

        return carry

    lax.fori_loop(1, n_ctx, earlier_block, 0)
    for head in range(heads):
        attended_ref[:, head * head_dim : (head + 1) * head_dim] = (
            sum_ref[head] / total_ref[head]
        ).astype(bf16)

    loads[0].wait()
    chunk = 512
    for start in range(0, width, chunk):
        part = jnp.dot(
            attended_ref[...], w_out[:, start : start + chunk], preferred_element_type=f32
        )
        rs_send[:, :, start : start + chunk] = part.astype(bf16).reshape(n_exp, own, chunk)

    def share(k):
        peer = lax.rem(e + k, n_exp)
        return remote(
            rs_send.at[peer],
            rs_recv.at[k],
            rs_send_sem.at[k],
            rs_recv_sem.at[k],
            {"exp": peer},
        )

    def start_of(copy_of):
        return lambda k: copy_of(k).start()

    def wait_recv_of(copy_of):
        return lambda k: copy_of(k).wait_recv()

    def wait_send_of(copy_of):
        return lambda k: copy_of(k).wait_send()

    each(1, n_exp, start_of(share))
    residual = tokens_ref[pl.ds(pl.multiple_of(e * own, own), own), :].astype(f32) + rs_send[e].astype(f32)
    each(1, n_exp, wait_recv_of(share))
    for k in range(1, n_exp):
        residual = residual + rs_recv[k].astype(f32)

    square = jnp.mean(residual * residual, axis=-1, keepdims=True)
    normed = (residual * lax.rsqrt(square + epsilon) * gain_ref[...]).astype(bf16)
    outgoing = jnp.dot(in_slot, normed, preferred_element_type=f32)

    def packed(rows):
        parts = [
            rows[:, p * piece : (p + 1) * piece].reshape(-1, ROWS, piece) for p in range(pieces)
        ]
        if pieces == 1:
            parts.append(jnp.zeros_like(parts[0]))
        return jnp.concatenate(parts, axis=1).astype(bf16)

    def unpacked(rows, p):
        return rows[:, p * ROWS : (p + 1) * ROWS, :].reshape(-1, piece)

    for block in range(n_ctx):
        rows_send[block * n_exp : (block + 1) * n_exp] = packed(
            outgoing[:, block * columns : (block + 1) * columns]
        )

    def to_all(send, recv, send_sem, recv_sem):
        def copy_of(k):
            peer = lax.rem(me + k, devices)
            return remote(
                send.at[peer],
                recv.at[me],
                send_sem.at[k],
                recv_sem.at[k],
                {"ctx": peer // n_exp, "exp": lax.rem(peer, n_exp)},
            )

        return copy_of

    dispatch = to_all(rows_send, rows_recv, rows_send_sem, rows_recv_sem)
    each(1, devices, start_of(dispatch))
    rows_recv[me] = rows_send[me]
    loads[1].wait()
    loads[2].wait()
    each(1, devices, wait_recv_of(dispatch))
    used = n_exp * CAP
    slot = lax.broadcasted_iota(jnp.int32, (used, n_exp * ROWS), 1)
    place = lax.rem(slot, ROWS)
    keep = jnp.logical_and(
        lax.broadcasted_iota(jnp.int32, slot.shape, 0) == (slot // ROWS) * CAP + place, place < CAP
    )
    keep = keep.astype(f32).astype(bf16)
    gate = None
    for p in range(pieces):
        rows = jnp.concatenate(
            [
                jnp.dot(
                    keep,
                    unpacked(
                        rows_recv[block * n_exp : (block + 1) * n_exp].astype(f32), p
                    ).astype(bf16),
                    preferred_element_type=f32,
                )
                for block in range(n_ctx)
            ],
            axis=0,
        ).astype(bf16)
        gate_p = jnp.dot(
            rows, w_gate[p * piece : (p + 1) * piece, :], preferred_element_type=f32
        )
        up_p = jnp.dot(rows, w_up[p * piece : (p + 1) * piece, :], preferred_element_type=f32)
        gate, up = (gate_p, up_p) if gate is None else (gate + gate_p, up + up_p)
    for block in range(n_ctx):
        mine = slice(block * used, (block + 1) * used)
        part_send[block] = jnp.concatenate([gate[mine], up[mine]], axis=0).astype(bf16)

    def partial(k):
        peer = lax.rem(c + k, n_ctx)
        return remote(
            part_send.at[peer],
            part_recv.at[k],
            part_send_sem.at[k],
            part_recv_sem.at[k],
            {"ctx": peer},
        )

    each(1, n_ctx, start_of(partial))
    summed = part_send[c].astype(f32)
    each(1, n_ctx, wait_recv_of(partial))
    for k in range(1, n_ctx):
        summed = summed + part_recv[k].astype(f32)
    gate = summed[:used]
    hidden = gate / (1.0 + jnp.exp(-gate)) * summed[used:]
    half = hidden_width // 2
    hidden_ref[c] = jnp.concatenate([hidden[:, :half], hidden[:, half:]], axis=0).astype(bf16)

    def hidden_copy(k):
        return remote(
            hidden_ref.at[c],
            hidden_ref.at[c],
            hidden_send_sem.at[k],
            hidden_recv_sem.at[k],
            {"ctx": lax.rem(c + k, n_ctx)},
        )

    each(1, n_ctx, start_of(hidden_copy))
    loads[3].wait()
    each(1, n_ctx, wait_recv_of(hidden_copy))
    hidden = hidden_ref[...].astype(f32)
    expert_out = None
    for p in range(2):
        rows = hidden[:, p * used : (p + 1) * used, :].reshape(-1, half).astype(bf16)
        out_p = jnp.dot(rows, w_down[p * half : (p + 1) * half, :], preferred_element_type=f32)
        expert_out = out_p if expert_out is None else expert_out + out_p
    for block in range(n_ctx):
        rows = expert_out[block * used : (block + 1) * used].astype(bf16)
        rows = lax.dot_general(keep, rows, (((0,), (0,)), ((), ())), preferred_element_type=f32)
        back_send[block * n_exp : (block + 1) * n_exp] = packed(rows)
    back = to_all(back_send, back_recv, back_send_sem, back_recv_sem)
    each(1, devices, start_of(back))
    back_recv[me] = back_send[me]
    each(1, devices, wait_recv_of(back))
    for block in range(n_ctx):
        rows = back_recv[block * n_exp : (block + 1) * n_exp].astype(f32)
        for p in range(pieces):
            begin = block * columns + p * piece
            mixed = jnp.dot(
                combine_ref[...],
                unpacked(rows, p),
                precision=lax.Precision.HIGHEST,
                preferred_element_type=f32,
            )
            out_ref[:, begin : begin + piece] = (
                residual[:, begin : begin + piece] + mixed
            ).astype(bf16)

    def sent_block(step, carry):
        @pl.when(jnp.logical_and(step <= c, c + 1 < n_ctx))
        def _():
            for part in range(groups):
                hop(c - step, part).wait_send()

        return carry

    lax.fori_loop(0, n_ctx, sent_block, 0)
    each(1, n_exp, wait_send_of(share))
    each(1, devices, wait_send_of(dispatch))
    each(1, n_ctx, wait_send_of(partial))
    each(1, n_ctx, wait_send_of(hidden_copy))
    each(1, devices, wait_send_of(back))


def body(
    tokens,
    positions,
    attn_gain,
    w_qkv,
    w_out,
    moe_gain,
    expert_ids,
    gate_probs,
    w_gate,
    w_up,
    w_down,
):
    seq_dev = tokens.shape[0]
    width = tokens.shape[1]
    head_dim = w_out.shape[1]
    heads_here = w_out.shape[0]
    n_ctx = lax.axis_size("ctx")
    n_exp = lax.axis_size("exp")
    devices = n_ctx * n_exp
    normed = rms_norm(tokens, attn_gain).astype(jnp.bfloat16)
    projected = jnp.einsum("sd,dhc->hsc", normed, w_qkv, preferred_element_type=jnp.float32)
    cosines, sines = rotary_tables(positions, head_dim)
    own = seq_dev // n_exp

    columns = width // n_ctx
    pieces = 2 if columns % 256 == 0 else 1
    piece = columns // pieces
    groups = heads_here
    hidden_width = w_gate.shape[2]
    bf16 = jnp.bfloat16
    vmem = pl.BlockSpec(memory_space=pltpu.VMEM)
    anywhere = pl.BlockSpec(memory_space=pl.ANY)
    dma = pltpu.SemaphoreType.DMA
    return pl.pallas_call(
        functools.partial(layer_kernel, n_ctx, n_exp, pieces, groups),
        out_shape=jax.ShapeDtypeStruct((own, width), bf16),
        in_specs=[vmem] * 7 + [anywhere] * 4,
        out_specs=vmem,
        scratch_shapes=[
            pltpu.VMEM((own, n_exp * ROWS), jnp.float32),
            pltpu.VMEM((heads_here, seq_dev, head_dim), bf16),
            pltpu.VMEM((n_ctx, 2 * heads_here, seq_dev, head_dim), bf16),
            pltpu.VMEM((heads_here, seq_dev, 1), jnp.float32),
            pltpu.VMEM((heads_here, seq_dev, 1), jnp.float32),
            pltpu.VMEM((heads_here, seq_dev, head_dim), jnp.float32),
            pltpu.VMEM((seq_dev, heads_here * head_dim), bf16),
            pltpu.VMEM((heads_here * head_dim, width), bf16),
            pltpu.VMEM(w_gate.shape[1:], bf16),
            pltpu.VMEM(w_up.shape[1:], bf16),
            pltpu.VMEM(w_down.shape[1:], bf16),
            pltpu.VMEM((n_exp, own, width), bf16),
            pltpu.VMEM((n_exp, own, width), bf16),
            pltpu.VMEM((devices, 2 * ROWS, piece), bf16),
            pltpu.VMEM((devices, 2 * ROWS, piece), bf16),
            pltpu.VMEM((n_ctx, 2 * n_exp * CAP, hidden_width), bf16),
            pltpu.VMEM((n_ctx, 2 * n_exp * CAP, hidden_width), bf16),
            pltpu.VMEM((n_ctx, 2 * n_exp * CAP, hidden_width // 2), bf16),
            pltpu.VMEM((devices, 2 * ROWS, piece), bf16),
            pltpu.VMEM((devices, 2 * ROWS, piece), bf16),
            dma((4,)),
            dma((n_ctx, groups)),
            dma((n_ctx, groups)),
            dma((n_exp,)),
            dma((n_exp,)),
            dma((devices,)),
            dma((devices,)),
            dma((n_ctx,)),
            dma((n_ctx,)),
            dma((n_ctx,)),
            dma((n_ctx,)),
            dma((devices,)),
            dma((devices,)),
        ],
        compiler_params=pltpu.CompilerParams(
            collective_id=0, has_side_effects=True, vmem_limit_bytes=60 * 1024 * 1024
        ),
    )(
        projected,
        cosines,
        sines,
        tokens,
        moe_gain.reshape(1, width),
        expert_ids.T,
        gate_probs.T,
        w_out.reshape(heads_here * head_dim, width),
        w_gate[0],
        w_up[0],
        w_down[0],
    )


def solution(mesh):
    return jax.shard_map(
        body,
        mesh=mesh,
        in_specs=(
            P(("groups", "ctx"), None),
            P(("groups", "ctx")),
            P(),
            P(None, "exp", None),
            P("exp", None, None),
            P(),
            P(("groups", "ctx", "exp"), None),
            P(("groups", "ctx", "exp"), None),
            P("exp", "ctx", None),
            P("exp", "ctx", None),
            P("exp", None, "ctx"),
        ),
        out_specs=P(("groups", "ctx", "exp"), None),
        check_vma=False,
    )
```
